32 devices in a mesh: groups: 2 (over x), tenant: 16 (over z, y, core).
Axes of the slice: x: 2, y: 2, z: 4, core: 2. Of those that a mesh axis runs over, the one named last changes fastest.
Arguments:
- tokens: bfloat16 [4096, 8192], P(('groups', 'tenant')), parts along dimension 0, may hold values from -6 to 6
- cotangent: bfloat16 [4096, 8192], P(('groups', 'tenant')), parts along dimension 0, may hold values from -6 to 6
- down_a: float32 [16, 64, 8192], P('tenant'), may hold values from -0.0625 to 0.0625
- up_b: float32 [16, 64, 8192], P('tenant'), may hold values from -0.0625 to 0.0625
- block_tenant: int32 [32], P('groups'), parts along dimension 0, may hold values from 0 to 15, as said below
- tenant_slot: int32 [16], replicated, may hold values from 0 to 15, each once
Outputs:
- grad_tokens: bfloat16 [4096, 8192], P(('groups', 'tenant')), parts along dimension 0
- grad_down: bfloat16 [32, 64, 8192], P(('groups', 'tenant')), parts along dimension 0
- grad_up: bfloat16 [32, 64, 8192], P(('groups', 'tenant')), parts along dimension 0
The draws below stay inside these ranges and needn't reach their ends.
There are 2 independent parts, one for each index of `groups`. The reference program is written for one: setup_inputs(seed, part) draws one part's arguments, and reference() takes and returns one part's arrays. A program takes and returns all parts, laid end to end along the dimension named above; an argument that names none is the same for every part. Nothing has to cross between parts.
Inputs may be any that keep to these rules, and one draw needn't show every extreme that they name: `block_tenant`: no tenant owns more than 4 blocks, and one tenant owns exactly 4. `tenant_slot`: each tenant has its own storage row.
All inputs are finite; a program needn't handle non-finite values.
Results may differ from the reference program's by a relative error of at most 0.0064.
Values may be sent and summed in bfloat16 or wider, within the bound.
A program may use at most 128 MiB of HBM per device.

```python
import jax
import jax.numpy as jnp
from jax import lax

D = 8192
R = 64
BLOCK = 128
MOST = 4
TENANTS = 16
BLOCKS = 16
TOKENS = 2048


def draw_block_tenant(key, part):
    key = jax.random.fold_in(key, 11)
    key_hot, key_rest, key_order = jax.random.split(key, 3)
    hottest = jax.random.randint(key_hot, (), 0, TENANTS, dtype=jnp.int32)
    others = jnp.arange((TENANTS - 1) * MOST, dtype=jnp.int32) // MOST
    others = jax.random.permutation(key_rest, others)[:BLOCKS - MOST]
    others = others + (others >= hottest).astype(jnp.int32)
    labels = jnp.concatenate([jnp.full((MOST,), hottest, jnp.int32), others])
    return jax.random.permutation(key_order, labels).astype(jnp.int32)


def level_of(own_key, dims, cuts, smallest, largest):
    level, own = 1.0, jax.random.fold_in(own_key, 6)
    for axis_at, parts in cuts:
        heights = jnp.exp(jax.random.uniform(jax.random.fold_in(own, axis_at), (parts,), jnp.float32, smallest / len(cuts), largest / len(cuts)))
        level = level * jnp.repeat(heights, dims[axis_at] // parts).reshape([-1 if axis == axis_at else 1 for axis in range(len(dims))])
    return level


def normal_values(key, extent, spread, bound, shards=(), kind=jnp.bfloat16):
    level = level_of(key, extent, shards, -0.22, 0.18) if shards else 1.0
    result = jax.random.normal(key, extent, jnp.float32) * spread * level
    return jnp.minimum(jnp.maximum(result, -bound), bound).astype(kind)


def setup_inputs(seed: int = 0, part: int = 0) -> dict:
    streams_of = jax.random.split(jax.random.key(seed), 7)
    part_splits = jax.random.split(jax.random.fold_in(streams_of[6], part), 7)
    return {
        "tokens": normal_values(part_splits[0], (TOKENS, D), 1.0, 6.0, ((0, 16),)),
        "cotangent": normal_values(part_splits[1], (TOKENS, D), 1.0, 6.0, ((0, 16),)),
        "down_a": normal_values(streams_of[2], (TENANTS, R, D), D ** -0.5, 0.0625, ((0, 16),), jnp.float32),
        "up_b": normal_values(streams_of[3], (TENANTS, R, D), D ** -0.5, 0.0625, ((0, 16),), jnp.float32),
        "block_tenant": draw_block_tenant(jax.random.fold_in(jax.random.fold_in(streams_of[6], part), 71), part),
        "tenant_slot": jax.random.permutation(streams_of[5], TENANTS).astype(jnp.int32),
    }


adapter_scale = 2.0


def reference(tokens, cotangent, down_a, up_b, block_tenant, tenant_slot):
    down_low = down_a.astype(jnp.bfloat16)
    up_low = up_b.astype(jnp.bfloat16)
    slot_of_block = tenant_slot[block_tenant].astype(jnp.int32)
    token_blocks = tokens.reshape(BLOCKS, BLOCK, D)
    cotan_blocks = cotangent.reshape(BLOCKS, BLOCK, D)

    def one_block(carry, item):
        grad_down, grad_up = carry
        x_block, gradient_block, slot = item
        down_one = lax.dynamic_index_in_dim(down_low, slot, 0, keepdims=False)
        single_up_weight = lax.dynamic_index_in_dim(up_low, slot, 0, keepdims=False)
        forward_rank_rows = jnp.dot(x_block, down_one.T, preferred_element_type=jnp.float32).astype(jnp.bfloat16)
        backward_rank_rows = (adapter_scale * jnp.dot(gradient_block, single_up_weight.T, preferred_element_type=jnp.float32)).astype(jnp.bfloat16)
        grad_x = jnp.dot(backward_rank_rows, down_one, preferred_element_type=jnp.float32).astype(jnp.bfloat16)
        term_down = jnp.dot(backward_rank_rows.T, x_block, preferred_element_type=jnp.float32)
        up_term_value = adapter_scale * jnp.dot(forward_rank_rows.T, gradient_block, preferred_element_type=jnp.float32)
        grad_down = grad_down.at[slot].add(term_down)
        grad_up = grad_up.at[slot].add(up_term_value)
        return (grad_down, grad_up), grad_x

    start = (jnp.zeros((TENANTS, R, D), jnp.float32), jnp.zeros((TENANTS, R, D), jnp.float32))
    (grad_down, grad_up), grad_blocks = lax.scan(one_block, start, (token_blocks, cotan_blocks, slot_of_block))
    return grad_blocks.reshape(TOKENS, D), grad_down.astype(jnp.bfloat16), grad_up.astype(jnp.bfloat16)
```

```python
import functools

import jax
import jax.numpy as jnp
from jax import lax
from jax.experimental import pallas as pl
from jax.experimental.pallas import tpu as pltpu
from jax.sharding import PartitionSpec as P

adapter_scale = 2.0
MOST = 4
MESH = pl.DeviceIdType.MESH


def wait_bytes(ref, sem):
    pltpu.make_async_copy(ref, ref, sem).wait()


def kernel(
    groups, n,
    tok_h, cot_h, down_h, up_h, bt_v, ts_s,
    gt_h, gd_h, gu_h,
    raw, low, recv1_u, recv1_d, stage2, recv2, stage3, recv3_u, recv3_d, stage4, tok_v, cot_v, gt_v, bt_all, bt_s,
    in_sem, bt_send, bt_recv, send_sem, recv_sem, gt_sem,
):
    recv1, recv3 = (recv1_u, recv1_d), (recv3_u, recv3_d)
    width = tok_h.shape[1]
    w = width // n
    ng = n // groups
    g = lax.axis_index("groups")
    me = lax.axis_index("tenant")
    side = me // ng
    r_me = me % ng
    c_me = g * ng + r_me

    def cols(c):
        return pl.ds(pl.multiple_of(c * w, w), w)

    share = pl.ds(pl.multiple_of(g * (ng * w), ng * w), ng * w)
    loads = [
        pltpu.make_async_copy(up_h.at[0, :, share], raw.at[0], in_sem.at[0]),
        pltpu.make_async_copy(down_h.at[0, :, share], raw.at[1], in_sem.at[1]),
        pltpu.make_async_copy(cot_h, cot_v, in_sem.at[2]),
        pltpu.make_async_copy(tok_h, tok_v, in_sem.at[3]),
    ]
    for load in loads:
        load.start()

    barrier = pltpu.get_barrier_semaphore()

    @pl.loop(1, n)
    def _(k):
        pl.semaphore_signal(barrier, inc=1, device_id=(g, (me + k) % n), device_id_type=MESH)

    for dg in range(1, groups):
        @pl.loop(0, ng)
        def _(r):
            pl.semaphore_signal(
                barrier, inc=1, device_id=((g + dg) % groups, side * ng + r), device_id_type=MESH
            )

    def cast(q):
        loads[q].wait()

        @pl.loop(0, ng)
        def _(r):
            low[q, r] = raw[q, :, cols(r)].astype(jnp.bfloat16)

    cast(0)
    for q in range(2):
        recv3[q][n] = jnp.zeros(recv3[q].shape[1:], jnp.bfloat16)
    pl.semaphore_wait(barrier, n - 1 + (groups - 1) * ng)

    own_map = pltpu.make_async_copy(bt_v, bt_all.at[g], bt_recv)
    own_map.start()
    for dg in range(1, groups):
        pltpu.make_async_remote_copy(
            src_ref=bt_v, dst_ref=bt_all.at[g], send_sem=bt_send.at[dg], recv_sem=bt_recv,
            device_id=((g + dg) % groups, me), device_id_type=MESH,
        ).start()

    def send(here, src, dst, hop, q, device):
        @pl.when(here)
        def _():
            pltpu.make_async_copy(src, dst, recv_sem.at[hop, q]).start()

        @pl.when(jnp.logical_not(here))
        def _():
            pltpu.make_async_remote_copy(
                src_ref=src, dst_ref=dst, send_sem=send_sem.at[hop, q], recv_sem=recv_sem.at[hop, q],
                device_id=device, device_id_type=MESH,
            ).start()

    def hop1(q):
        @pl.loop(0, n)
        def _(k):
            to = (me + n - 1 - k) % n
            send(to == me, low.at[q, to % ng], recv1[q].at[me], 0, q, (g, to))

    hop1(0)
    cast(1)
    hop1(1)

    wait_bytes(bt_all, bt_recv)
    to_scalar = pltpu.make_async_copy(bt_all, bt_s, in_sem.at[4])
    to_scalar.start()
    to_scalar.wait()

    def hop2(q):
        wait_bytes(recv1[q], recv_sem.at[0, q])
        for dg in range(groups):
            to_g = (g + dg) % groups

            @pl.loop(0, ng)
            def _(k):
                to = side * ng + (r_me + k) % ng
                slot = ts_s[bt_s[to_g, 0, to]]
                at = dg * ng + k
                stage2[q, at] = recv1[q][slot]
                here = (k == 0) if dg == 0 else (k < 0)
                send(here, stage2.at[q, at], recv2.at[q, c_me], 1, q, (to_g, to))

    hop2(0)
    hop2(1)

    block_rows = tok_h.shape[0]
    rank = down_h.shape[1]

    def rank_rows(rows_v, q):
        def step(c, total):
            return total + lax.dot_general(
                rows_v[:, cols(c)], recv2[q, c], (((1,), (1,)), ((), ())),
                preferred_element_type=jnp.float32,
            )
        return lax.fori_loop(0, n, step, jnp.zeros((block_rows, rank), jnp.float32))

    def hop3(q, left, rows_v, scale):
        @pl.loop(0, n)
        def _(k):
            to = (me + n - 1 - k) % n
            term = scale * jnp.dot(left, rows_v[:, cols(to)], preferred_element_type=jnp.float32)
            stage3[q, to] = term.astype(jnp.bfloat16)
            send(to == me, stage3.at[q, to], recv3[q].at[me], 2, q, (g, to))

    wait_bytes(recv2.at[0], recv_sem.at[1, 0])
    loads[2].wait()
    loads[3].wait()
    backward = adapter_scale * rank_rows(cot_v, 0)
    hop3(0, backward.T.astype(jnp.bfloat16), tok_v, 1.0)
    backward = backward.astype(jnp.bfloat16)

    wait_bytes(recv2.at[1], recv_sem.at[1, 1])
    forward = rank_rows(tok_v, 1)
    hop3(1, forward.T.astype(jnp.bfloat16), cot_v, adapter_scale)

    @pl.loop(0, n)
    def _(c):
        gt_v[:, cols(c)] = jnp.dot(
            backward, recv2[1, c], preferred_element_type=jnp.float32
        ).astype(jnp.bfloat16)

    gt_out = pltpu.make_async_copy(gt_v, gt_h, gt_sem)
    gt_out.start()

    def hop4(q, out_h):
        wait_bytes(recv3[q].at[pl.ds(0, n)], recv_sem.at[2, q])

        @pl.loop(0, n)
        def _(k):
            to = (me + n - 1 - k) % n

            def find(b, found):
                hit = ts_s[bt_s[g, 0, b]] == to
                later = (b,) + found[:-1]
                return tuple(jnp.where(hit, new, old) for new, old in zip(later, found))

            found = lax.fori_loop(0, n, find, (jnp.int32(n),) * MOST)
            total = recv3[q][found[0]].astype(jnp.float32)
            for b in found[1:]:
                total += recv3[q][b].astype(jnp.float32)
            stage4[q, to] = total.astype(jnp.bfloat16)
            send(to == me, stage4.at[q, to], out_h.at[0, :, cols(me)], 3, q, (g, to))

    hop4(0, gd_h)
    hop4(1, gu_h)

    wait_bytes(gd_h, recv_sem.at[3, 0])
    wait_bytes(gu_h, recv_sem.at[3, 1])
    for hop, source in enumerate((stage2, stage2, stage3, stage4)):
        for q in range(2):
            wait_bytes(source.at[q, pl.ds(0, n - 1)], send_sem.at[hop, q])
    for dg in range(1, groups):
        wait_bytes(bt_v, bt_send.at[dg])
    gt_out.wait()


def shards(groups, n, tokens, cotangent, down_a, up_b, block_tenant, tenant_slot):
    block_rows, width = tokens.shape
    rank = down_a.shape[1]
    w = width // n
    ng = n // groups
    assert down_a.shape[0] == 1 and block_tenant.shape[0] == n
    bt = jnp.zeros((8, 128), jnp.int32).at[0, :n].set(block_tenant)
    low = jnp.bfloat16
    whole = pl.BlockSpec(memory_space=pl.ANY)
    return pl.pallas_call(
        functools.partial(kernel, groups, n),
        out_shape=(
            jax.ShapeDtypeStruct((block_rows, width), low),
            jax.ShapeDtypeStruct((1, rank, width), low),
            jax.ShapeDtypeStruct((1, rank, width), low),
        ),
        in_specs=[whole] * 4 + [
            pl.BlockSpec(memory_space=pltpu.VMEM),
            pl.BlockSpec(memory_space=pltpu.SMEM),
        ],
        out_specs=(whole,) * 3,
        scratch_shapes=[
            pltpu.VMEM((2, rank, ng * w), jnp.float32),
            pltpu.VMEM((2, ng, rank, w), low),
            pltpu.VMEM((n, rank, w), low),
            pltpu.VMEM((n, rank, w), low),
            pltpu.VMEM((2, n, rank, w), low),
            pltpu.VMEM((2, n, rank, w), low),
            pltpu.VMEM((2, n, rank, w), low),
            pltpu.VMEM((n + 1, rank, w), low),
            pltpu.VMEM((n + 1, rank, w), low),
            pltpu.VMEM((2, n, rank, w), low),
            pltpu.VMEM((block_rows, width), low),
            pltpu.VMEM((block_rows, width), low),
            pltpu.VMEM((block_rows, width), low),
            pltpu.VMEM((groups, 8, 128), jnp.int32),
            pltpu.SMEM((groups, 8, 128), jnp.int32),
            pltpu.SemaphoreType.DMA((5,)),
            pltpu.SemaphoreType.DMA((groups,)),
            pltpu.SemaphoreType.DMA,
            pltpu.SemaphoreType.DMA((4, 2)),
            pltpu.SemaphoreType.DMA((4, 2)),
            pltpu.SemaphoreType.DMA,
        ],
        compiler_params=pltpu.CompilerParams(
            collective_id=0, has_side_effects=True, vmem_limit_bytes=40 * 2**20
        ),
    )(tokens, cotangent, down_a, up_b, bt, tenant_slot)


def solution(mesh):
    groups, n = mesh.shape["groups"], mesh.shape["tenant"]
    return jax.shard_map(
        functools.partial(shards, groups, n),
        mesh=mesh,
        in_specs=(
            P(("groups", "tenant"), None),
            P(("groups", "tenant"), None),
            P("tenant", None, None),
            P("tenant", None, None),
            P("groups"),
            P(),
        ),
        out_specs=(
            P(("groups", "tenant"), None),
            P(("groups", "tenant"), None, None),
            P(("groups", "tenant"), None, None),
        ),
        check_vma=False,
    )
```

```python
import functools

import jax
import jax.numpy as jnp
from jax import lax
from jax.experimental import pallas as pl
from jax.experimental.pallas import tpu as pltpu
from jax.sharding import PartitionSpec as P

adapter_scale = 2.0
MOST = 4
MESH = pl.DeviceIdType.MESH


def wait_bytes(ref, sem):
    pltpu.make_async_copy(ref, ref, sem).wait()


def kernel(
    groups, n, most_sent,
    tok_h, cot_h, down_h, up_h, slot_s,
    gt_h, gd_h, gu_h,
    raw, low, recv1_u, recv1_d, stage2, recv2, stage3, recv3_u, recv3_d, stage4, recv4_u, recv4_d, stage5,
    tok_v, cot_v, gt_v, own_s, pack_s, got_s, found_s, rank_s,
    in_sem, send_sem, recv_sem, gt_sem,
):
    recv1, recv3, recv4 = (recv1_u, recv1_d), (recv3_u, recv3_d), (recv4_u, recv4_d)
    width = tok_h.shape[1]
    block_rows = tok_h.shape[0]
    rank = down_h.shape[1]
    w = width // n
    ng = n // groups
    g = lax.axis_index("groups")
    me = lax.axis_index("tenant")
    side = me // ng
    r_me = me % ng
    c_me = g * ng + r_me
    crossing = (groups - 1) * most_sent

    def cols(c):
        return pl.ds(pl.multiple_of(c * w, w), w)

    share = pl.ds(pl.multiple_of(g * (ng * w), ng * w), ng * w)
    loads = [
        pltpu.make_async_copy(up_h.at[0, :, share], raw.at[0], in_sem.at[0]),
        pltpu.make_async_copy(down_h.at[0, :, share], raw.at[1], in_sem.at[1]),
        pltpu.make_async_copy(cot_h, cot_v, in_sem.at[2]),
        pltpu.make_async_copy(tok_h, tok_v, in_sem.at[3]),
    ]
    for load in loads:
        load.start()

    barrier = pltpu.get_barrier_semaphore()

    @pl.loop(1, n)
    def _(k):
        pl.semaphore_signal(barrier, inc=1, device_id=(g, (me + k) % n), device_id_type=MESH)

    for dg in range(1, groups):
        @pl.loop(0, ng)
        def _(r):
            pl.semaphore_signal(
                barrier, inc=1, device_id=((g + dg) % groups, side * ng + r), device_id_type=MESH
            )

    def cast(q):
        loads[q].wait()

        @pl.loop(0, ng)
        def _(r):
            low[q, r] = raw[q, :, cols(r)].astype(jnp.bfloat16)

    cast(0)
    for q in range(2):
        recv3[q][n] = jnp.zeros((rank, w), jnp.bfloat16)
        recv4[q][crossing] = jnp.zeros((rank, w), jnp.bfloat16)
    pl.semaphore_wait(barrier, n - 1 + (groups - 1) * ng)

    def send(here, src, dst, hop, q, device):
        @pl.when(here)
        def _():
            pltpu.make_async_copy(src, dst, recv_sem.at[hop, q]).start()

        @pl.when(jnp.logical_not(here))
        def _():
            pltpu.make_async_remote_copy(
                src_ref=src, dst_ref=dst, send_sem=send_sem.at[hop, q], recv_sem=recv_sem.at[hop, q],
                device_id=device, device_id_type=MESH,
            ).start()

    def hop1(q):
        @pl.loop(0, n)
        def _(k):
            to = ((side + 1 + k // ng) % groups) * ng + (r_me + k) % ng
            send(to == me, low.at[q, to % ng], recv1[q].at[me], 0, q, (g, to))

    hop1(0)
    cast(1)
    hop1(1)

    def find(dg, t, base):
        def step(b, found):
            hit = slot_s[dg, base * ng + b] == t
            later = (((g + dg) % groups) * ng + b,) + found[:-1]
            return tuple(jnp.where(hit, new, old) for new, old in zip(later, found))
        return lax.fori_loop(0, ng, step, (jnp.int32(n),) * MOST)

    @pl.loop(0, n)
    def _(p):
        for i, b in enumerate(find(p // ng, side * ng + p % ng, side)):
            own_s[p * MOST + i] = b

    for i in range(MOST):
        found_s[n * MOST + i] = jnp.int32(n)
    for dh in range(1, groups):
        there, origin = (side + dh) % groups, (side + groups - dh) % groups

        def outgoing(p, count):
            found = find(p // ng, there * ng + p % ng, side)
            for i, b in enumerate(found):
                found_s[p * MOST + i] = b
            rank_s[p] = jnp.where(found[0] != n, count, -1)
            return count + jnp.where(found[0] != n, 1, 0)

        lax.fori_loop(0, n, outgoing, jnp.int32(0))

        @pl.loop(0, most_sent)
        def _(k):
            chosen = lax.fori_loop(
                0, n, lambda p, old: jnp.where(rank_s[p] == k, p, old), jnp.int32(n)
            )
            for i in range(MOST):
                pack_s[((dh - 1) * most_sent + k) * MOST + i] = found_s[chosen * MOST + i]

        def incoming(p, count):
            present = find(p // ng, side * ng + p % ng, origin)[0] != n
            got_s[(dh - 1) * n + p] = jnp.where(present, (dh - 1) * most_sent + count, crossing)
            return count + jnp.where(present, 1, 0)

        lax.fori_loop(0, n, incoming, jnp.int32(0))

    def over_side(body):
        for dg in range(groups):
            @pl.loop(0, ng)
            def _(k):
                r = (r_me + k) % ng
                body((k == 0) if dg == 0 else (k < 0), dg, (g + dg) % groups, r)

    def hop2(q):
        wait_bytes(recv1[q], recv_sem.at[0, q])

        def one(here, dg, to_g, r):
            to = side * ng + r
            at = dg * ng + r
            stage2[q, at] = recv1[q][slot_s[dg, to]]
            send(here, stage2.at[q, at], recv2.at[q, c_me], 1, q, (to_g, to))

        over_side(one)

    hop2(0)
    hop2(1)

    def rank_rows(rows_v, q):
        def step(c, total):
            return total + lax.dot_general(
                rows_v[:, cols(c)], recv2[q, c], (((1,), (1,)), ((), ())),
                preferred_element_type=jnp.float32,
            )
        return lax.fori_loop(0, n, step, jnp.zeros((block_rows, rank), jnp.float32))

    def hop3(q, left, rows_v, scale):
        def one(here, dg, to_g, r):
            c = to_g * ng + r
            term = scale * jnp.dot(left, rows_v[:, cols(c)], preferred_element_type=jnp.float32)
            stage3[q, c] = term.astype(jnp.bfloat16)
            send(here, stage3.at[q, c], recv3[q].at[c_me], 2, q, (to_g, side * ng + r))

        over_side(one)

    def block_sum(q, index_s, at):
        total = recv3[q][index_s[at]].astype(jnp.float32)
        for i in range(1, MOST):
            total += recv3[q][index_s[at + i]].astype(jnp.float32)
        return total

    def hop4(q):
        wait_bytes(recv3[q].at[pl.ds(0, n)], recv_sem.at[2, q])
        for dh in range(1, groups):
            to = ((side + dh) % groups) * ng + r_me

            @pl.loop(0, most_sent)
            def _(k):
                at = (dh - 1) * most_sent + k
                stage4[q, at] = block_sum(q, pack_s, at * MOST).astype(jnp.bfloat16)
                pltpu.make_async_remote_copy(
                    src_ref=stage4.at[q, at], dst_ref=recv4[q].at[at],
                    send_sem=send_sem.at[3, q], recv_sem=recv_sem.at[3, q],
                    device_id=(g, to), device_id_type=MESH,
                ).start()

    def hop5(q, out_h):
        if groups > 1:
            wait_bytes(recv4[q].at[pl.ds(0, crossing)], recv_sem.at[3, q])

        def one(here, dg, to_g, r):
            p = dg * ng + r
            total = block_sum(q, own_s, p * MOST)
            for dh in range(1, groups):
                total += recv4[q][got_s[(dh - 1) * n + p]].astype(jnp.float32)
            stage5[q, p] = total.astype(jnp.bfloat16)
            send(here, stage5.at[q, p], out_h.at[0, :, cols(c_me)], 4, q, (to_g, side * ng + r))

        over_side(one)

    wait_bytes(recv2.at[0], recv_sem.at[1, 0])
    loads[2].wait()
    loads[3].wait()
    backward = adapter_scale * rank_rows(cot_v, 0)
    hop3(0, backward.T.astype(jnp.bfloat16), tok_v, 1.0)
    backward = backward.astype(jnp.bfloat16)

    wait_bytes(recv2.at[1], recv_sem.at[1, 1])
    forward = rank_rows(tok_v, 1)
    hop3(1, forward.T.astype(jnp.bfloat16), cot_v, adapter_scale)
    hop4(0)

    @pl.loop(0, n)
    def _(c):
        gt_v[:, cols(c)] = jnp.dot(
            backward, recv2[1, c], preferred_element_type=jnp.float32
        ).astype(jnp.bfloat16)

    gt_out = pltpu.make_async_copy(gt_v, gt_h, gt_sem)
    gt_out.start()

    hop4(1)
    hop5(0, gd_h)
    hop5(1, gu_h)

    wait_bytes(gd_h, recv_sem.at[4, 0])
    wait_bytes(gu_h, recv_sem.at[4, 1])
    for hop, source in ((0, stage2), (1, stage2), (2, stage3), (4, stage5)):
        for q in range(2):
            wait_bytes(source.at[q, pl.ds(0, n - 1)], send_sem.at[hop, q])
    if groups > 1:
        for q in range(2):
            wait_bytes(stage4.at[q], send_sem.at[3, q])
    gt_out.wait()


def adapters(groups, n, most_sent, name, tokens, cotangent, down_a, up_b, slots):
    block_rows, width = tokens.shape
    rank = down_a.shape[1]
    w = width // n
    ng = n // groups
    crossing = (groups - 1) * most_sent
    low = jnp.bfloat16
    whole = pl.BlockSpec(memory_space=pl.ANY)
    return pl.pallas_call(
        functools.partial(kernel, groups, n, most_sent),
        out_shape=(
            jax.ShapeDtypeStruct((block_rows, width), low),
            jax.ShapeDtypeStruct((1, rank, width), low),
            jax.ShapeDtypeStruct((1, rank, width), low),
        ),
        in_specs=[whole] * 4 + [pl.BlockSpec(memory_space=pltpu.SMEM)],
        out_specs=(whole,) * 3,
        scratch_shapes=[
            pltpu.VMEM((2, rank, ng * w), jnp.float32),
            pltpu.VMEM((2, ng, rank, w), low),
            pltpu.VMEM((n, rank, w), low),
            pltpu.VMEM((n, rank, w), low),
            pltpu.VMEM((2, n, rank, w), low),
            pltpu.VMEM((2, n, rank, w), low),
            pltpu.VMEM((2, n, rank, w), low),
            pltpu.VMEM((n + 1, rank, w), low),
            pltpu.VMEM((n + 1, rank, w), low),
            pltpu.VMEM((2, max(crossing, 1), rank, w), low),
            pltpu.VMEM((crossing + 1, rank, w), low),
            pltpu.VMEM((crossing + 1, rank, w), low),
            pltpu.VMEM((2, n, rank, w), low),
            pltpu.VMEM((block_rows, width), low),
            pltpu.VMEM((block_rows, width), low),
            pltpu.VMEM((block_rows, width), low),
            pltpu.SMEM((n * MOST,), jnp.int32),
            pltpu.SMEM((max(crossing, 1) * MOST,), jnp.int32),
            pltpu.SMEM((max(groups - 1, 1) * n,), jnp.int32),
            pltpu.SMEM(((n + 1) * MOST,), jnp.int32),
            pltpu.SMEM((n,), jnp.int32),
            pltpu.SemaphoreType.DMA((4,)),
            pltpu.SemaphoreType.DMA((5, 2)),
            pltpu.SemaphoreType.DMA((5, 2)),
            pltpu.SemaphoreType.DMA,
        ],
        compiler_params=pltpu.CompilerParams(
            collective_id=name, has_side_effects=True, vmem_limit_bytes=56 * 2**20
        ),
    )(tokens, cotangent, down_a, up_b, slots)


def shards(groups, n, tokens, cotangent, down_a, up_b, block_tenant, tenant_slot):
    assert down_a.shape[0] == 1 and block_tenant.shape[0] == n
    ng = n // groups
    mine = tenant_slot[block_tenant]
    slots = jnp.stack([mine] + [
        lax.ppermute(mine, "groups", [((i + dg) % groups, i) for i in range(groups)])
        for dg in range(1, groups)
    ])
    hit = slots[:, :, None] == jnp.arange(n, dtype=jnp.int32)
    pairs = jnp.any(hit.reshape(groups, groups, ng, groups, ng), axis=2)
    apart = jnp.arange(groups)[:, None] != jnp.arange(groups)[None, :]
    most = jnp.max(jnp.sum(pairs & apart[None, :, :, None], axis=(0, 3), dtype=jnp.int32))
    sizes = sorted({n * 3 // 8, n // 2, n * 5 // 8, n})
    which = sum((most > size).astype(jnp.int32) for size in sizes[:-1])
    return lax.switch(
        which,
        [functools.partial(adapters, groups, n, size, i) for i, size in enumerate(sizes)],
        tokens, cotangent, down_a, up_b, slots,
    )


def solution(mesh):
    groups, n = mesh.shape["groups"], mesh.shape["tenant"]
    return jax.shard_map(
        functools.partial(shards, groups, n),
        mesh=mesh,
        in_specs=(
            P(("groups", "tenant"), None),
            P(("groups", "tenant"), None),
            P("tenant", None, None),
            P("tenant", None, None),
            P("groups"),
            P(),
        ),
        out_specs=(
            P(("groups", "tenant"), None),
            P(("groups", "tenant"), None, None),
            P(("groups", "tenant"), None, None),
        ),
        check_vma=False,
    )
```

```python
import functools

import jax
import jax.numpy as jnp
from jax import lax
from jax.experimental import pallas as pl
from jax.experimental.pallas import tpu as pltpu
from jax.sharding import PartitionSpec as P

adapter_scale = 2.0
MOST = 4
PIECES = 2
Q = 2 * PIECES
MESH = pl.DeviceIdType.MESH


def wait_bytes(ref, sem):
    pltpu.make_async_copy(ref, ref, sem).wait()


def kernel(
    groups, n, most_sent,
    tok_h, cot_h, down_h, up_h, slot_s,
    gt_h, gd_h, gu_h,
    raw, low, recv1, stage2, recv2, stage3, recv3, stage4, recv4, stage5,
    tok_v, cot_v, gt_v, own_s, pack_s, got_s, found_s, rank_s,
    in_sem, send_sem, recv_sem, gt_sem,
):
    width = tok_h.shape[1]
    block_rows = tok_h.shape[0]
    rank = down_h.shape[1]
    rows = rank // PIECES
    w = width // n
    ng = n // groups
    g = lax.axis_index("groups")
    me = lax.axis_index("tenant")
    side = me // ng
    r_me = me % ng
    c_me = g * ng + r_me
    crossing = (groups - 1) * most_sent

    def cols(c):
        return pl.ds(pl.multiple_of(c * w, w), w)

    share = pl.ds(pl.multiple_of(g * (ng * w), ng * w), ng * w)
    loads = [
        pltpu.make_async_copy(up_h.at[0, :, share], raw.at[0], in_sem.at[0]),
        pltpu.make_async_copy(down_h.at[0, :, share], raw.at[1], in_sem.at[1]),
        pltpu.make_async_copy(cot_h, cot_v, in_sem.at[2]),
        pltpu.make_async_copy(tok_h, tok_v, in_sem.at[3]),
    ]
    for load in loads:
        load.start()

    barrier = pltpu.get_barrier_semaphore()

    @pl.loop(1, n)
    def _(k):
        pl.semaphore_signal(barrier, inc=1, device_id=(g, (me + k) % n), device_id_type=MESH)

    for dg in range(1, groups):
        @pl.loop(0, ng)
        def _(r):
            pl.semaphore_signal(
                barrier, inc=1, device_id=((g + dg) % groups, side * ng + r), device_id_type=MESH
            )

    def cast(q):
        first = q % PIECES
        if first == 0:
            loads[q // PIECES].wait()

        @pl.loop(0, ng)
        def _(r):
            low[q, r] = raw[q // PIECES, pl.ds(first * rows, rows), cols(r)].astype(jnp.bfloat16)

    cast(0)
    for q in range(Q):
        recv3[q][n] = jnp.zeros((rows, w), jnp.bfloat16)
        recv4[q][crossing] = jnp.zeros((rows, w), jnp.bfloat16)
    pl.semaphore_wait(barrier, n - 1 + (groups - 1) * ng)

    def send(here, src, dst, hop, q, device):
        @pl.when(here)
        def _():
            pltpu.make_async_copy(src, dst, recv_sem.at[hop, q]).start()

        @pl.when(jnp.logical_not(here))
        def _():
            pltpu.make_async_remote_copy(
                src_ref=src, dst_ref=dst, send_sem=send_sem.at[hop, q], recv_sem=recv_sem.at[hop, q],
                device_id=device, device_id_type=MESH,
            ).start()

    def hop1(q):
        @pl.loop(0, n)
        def _(k):
            to = ((side + 1 + k // ng) % groups) * ng + (r_me + k) % ng
            send(to == me, low.at[q, to % ng], recv1[q].at[me], 0, q, (g, to))

    hop1(0)
    for q in range(1, Q):
        cast(q)
        hop1(q)

    def over_side(body):
        for dg in range(groups):
            @pl.loop(0, ng)
            def _(k):
                r = (r_me + k) % ng
                body((k == 0) if dg == 0 else (k < 0), dg, (g + dg) % groups, r)

    def hop2(q):
        wait_bytes(recv1[q], recv_sem.at[0, q])

        def one(here, dg, to_g, r):
            to = side * ng + r
            at = dg * ng + r
            stage2[q, at] = recv1[q][slot_s[dg, to]]
            send(here, stage2.at[q, at], recv2.at[q, c_me], 1, q, (to_g, to))

        over_side(one)

    hop2(0)

    def find(dg, t, base):
        def step(b, found):
            hit = slot_s[dg, base * ng + b] == t
            later = (((g + dg) % groups) * ng + b,) + found[:-1]
            return tuple(jnp.where(hit, new, old) for new, old in zip(later, found))
        return lax.fori_loop(0, ng, step, (jnp.int32(n),) * MOST)

    @pl.loop(0, n)
    def _(p):
        for i, b in enumerate(find(p // ng, side * ng + p % ng, side)):
            own_s[p * MOST + i] = b

    for i in range(MOST):
        found_s[n * MOST + i] = jnp.int32(n)
    for dh in range(1, groups):
        there, origin = (side + dh) % groups, (side + groups - dh) % groups

        def outgoing(p, count):
            found = find(p // ng, there * ng + p % ng, side)
            for i, b in enumerate(found):
                found_s[p * MOST + i] = b
            rank_s[p] = jnp.where(found[0] != n, count, -1)
            return count + jnp.where(found[0] != n, 1, 0)

        lax.fori_loop(0, n, outgoing, jnp.int32(0))

        @pl.loop(0, most_sent)
        def _(k):
            chosen = lax.fori_loop(
                0, n, lambda p, old: jnp.where(rank_s[p] == k, p, old), jnp.int32(n)
            )
            for i in range(MOST):
                pack_s[((dh - 1) * most_sent + k) * MOST + i] = found_s[chosen * MOST + i]

        def incoming(p, count):
            present = find(p // ng, side * ng + p % ng, origin)[0] != n
            got_s[(dh - 1) * n + p] = jnp.where(present, (dh - 1) * most_sent + count, crossing)
            return count + jnp.where(present, 1, 0)

        lax.fori_loop(0, n, incoming, jnp.int32(0))

    def rank_rows(rows_v, q):
        def step(c, total):
            return total + lax.dot_general(
                rows_v[:, cols(c)], recv2[q, c], (((1,), (1,)), ((), ())),
                preferred_element_type=jnp.float32,
            )
        return lax.fori_loop(0, n, step, jnp.zeros((block_rows, rows), jnp.float32))

    def hop3(q, left, rows_v, scale):
        def one(here, dg, to_g, r):
            c = to_g * ng + r
            term = scale * jnp.dot(left, rows_v[:, cols(c)], preferred_element_type=jnp.float32)
            stage3[q, c] = term.astype(jnp.bfloat16)
            send(here, stage3.at[q, c], recv3[q].at[c_me], 2, q, (to_g, side * ng + r))

        over_side(one)

    def block_sum(q, index_s, at):
        total = recv3[q][index_s[at]].astype(jnp.float32)
        for i in range(1, MOST):
            total += recv3[q][index_s[at + i]].astype(jnp.float32)
        return total

    def hop4(q):
        wait_bytes(recv3[q].at[pl.ds(0, n)], recv_sem.at[2, q])
        for dh in range(1, groups):
            to = ((side + dh) % groups) * ng + r_me

            @pl.loop(0, most_sent)
            def _(k):
                at = (dh - 1) * most_sent + k
                stage4[q, at] = block_sum(q, pack_s, at * MOST).astype(jnp.bfloat16)
                pltpu.make_async_remote_copy(
                    src_ref=stage4.at[q, at], dst_ref=recv4[q].at[at],
                    send_sem=send_sem.at[3, q], recv_sem=recv_sem.at[3, q],
                    device_id=(g, to), device_id_type=MESH,
                ).start()

    def home(q):
        out_h = gu_h if q >= PIECES else gd_h
        return out_h.at[0, pl.ds(q % PIECES * rows, rows)]

    def hop5(q):
        if groups > 1:
            wait_bytes(recv4[q].at[pl.ds(0, crossing)], recv_sem.at[3, q])

        def one(here, dg, to_g, r):
            p = dg * ng + r
            total = block_sum(q, own_s, p * MOST)
            for dh in range(1, groups):
                total += recv4[q][got_s[(dh - 1) * n + p]].astype(jnp.float32)
            stage5[q, p] = total.astype(jnp.bfloat16)
            send(here, stage5.at[q, p], home(q).at[:, cols(c_me)], 4, q, (to_g, side * ng + r))

        over_side(one)

    backward = []

    def ranks(q):
        wait_bytes(recv2.at[q], recv_sem.at[1, q])
        if q == 0:
            loads[2].wait()
            loads[3].wait()
        if q < PIECES:
            found = adapter_scale * rank_rows(cot_v, q)
            backward.append(found.astype(jnp.bfloat16))
            hop3(q, found.T.astype(jnp.bfloat16), tok_v, 1.0)
        else:
            hop3(q, rank_rows(tok_v, q).T.astype(jnp.bfloat16), cot_v, adapter_scale)

    gt_out = pltpu.make_async_copy(gt_v, gt_h, gt_sem)
    for at in range(Q + 3):
        if 0 < at < Q:
            hop2(at)
        if 0 <= at - 1 < Q:
            ranks(at - 1)
        if 0 <= at - 2 < Q:
            hop4(at - 2)
        if at == Q:
            @pl.loop(0, n)
            def _(c):
                total = jnp.zeros((block_rows, w), jnp.float32)
                for i in range(PIECES):
                    total += jnp.dot(
                        backward[i], recv2[PIECES + i, c], preferred_element_type=jnp.float32
                    )
                gt_v[:, cols(c)] = total.astype(jnp.bfloat16)

            gt_out.start()
        if 0 <= at - 3 < Q:
            hop5(at - 3)

    for q in range(Q):
        wait_bytes(home(q), recv_sem.at[4, q])
    for hop, source in ((0, stage2), (1, stage2), (2, stage3), (4, stage5)):
        for q in range(Q):
            wait_bytes(source.at[q, pl.ds(0, n - 1)], send_sem.at[hop, q])
    if groups > 1:
        for q in range(Q):
            wait_bytes(stage4.at[q], send_sem.at[3, q])
    gt_out.wait()


def adapters(groups, n, most_sent, name, tokens, cotangent, down_a, up_b, slots):
    block_rows, width = tokens.shape
    rank = down_a.shape[1]
    rows = rank // PIECES
    w = width // n
    ng = n // groups
    crossing = (groups - 1) * most_sent
    low = jnp.bfloat16
    whole = pl.BlockSpec(memory_space=pl.ANY)
    return pl.pallas_call(
        functools.partial(kernel, groups, n, most_sent),
        out_shape=(
            jax.ShapeDtypeStruct((block_rows, width), low),
            jax.ShapeDtypeStruct((1, rank, width), low),
            jax.ShapeDtypeStruct((1, rank, width), low),
        ),
        in_specs=[whole] * 4 + [pl.BlockSpec(memory_space=pltpu.SMEM)],
        out_specs=(whole,) * 3,
        scratch_shapes=[
            pltpu.VMEM((2, rank, ng * w), jnp.float32),
            pltpu.VMEM((Q, ng, rows, w), low),
            [pltpu.VMEM((n, rows, w), low)] * Q,
            pltpu.VMEM((Q, n, rows, w), low),
            pltpu.VMEM((Q, n, rows, w), low),
            pltpu.VMEM((Q, n, rows, w), low),
            [pltpu.VMEM((n + 1, rows, w), low)] * Q,
            pltpu.VMEM((Q, max(crossing, 1), rows, w), low),
            [pltpu.VMEM((crossing + 1, rows, w), low)] * Q,
            pltpu.VMEM((Q, n, rows, w), low),
            pltpu.VMEM((block_rows, width), low),
            pltpu.VMEM((block_rows, width), low),
            pltpu.VMEM((block_rows, width), low),
            pltpu.SMEM((n * MOST,), jnp.int32),
            pltpu.SMEM((max(crossing, 1) * MOST,), jnp.int32),
            pltpu.SMEM((max(groups - 1, 1) * n,), jnp.int32),
            pltpu.SMEM(((n + 1) * MOST,), jnp.int32),
            pltpu.SMEM((n,), jnp.int32),
            pltpu.SemaphoreType.DMA((4,)),
            pltpu.SemaphoreType.DMA((5, Q)),
            pltpu.SemaphoreType.DMA((5, Q)),
            pltpu.SemaphoreType.DMA,
        ],
        compiler_params=pltpu.CompilerParams(
            collective_id=name, has_side_effects=True, vmem_limit_bytes=56 * 2**20
        ),
    )(tokens, cotangent, down_a, up_b, slots)


def shards(groups, n, tokens, cotangent, down_a, up_b, block_tenant, tenant_slot):
    assert down_a.shape[0] == 1 and block_tenant.shape[0] == n
    ng = n // groups
    mine = tenant_slot[block_tenant]
    slots = jnp.stack([mine] + [
        lax.ppermute(mine, "groups", [((i + dg) % groups, i) for i in range(groups)])
        for dg in range(1, groups)
    ])
    hit = slots[:, :, None] == jnp.arange(n, dtype=jnp.int32)
    pairs = jnp.any(hit.reshape(groups, groups, ng, groups, ng), axis=2)
    apart = jnp.arange(groups)[:, None] != jnp.arange(groups)[None, :]
    most = jnp.max(jnp.sum(pairs & apart[None, :, :, None], axis=(0, 3), dtype=jnp.int32))
    sizes = sorted({n // 2, n * 5 // 8, n})
    which = sum((most > size).astype(jnp.int32) for size in sizes[:-1])
    return lax.switch(
        which,
        [functools.partial(adapters, groups, n, size, i) for i, size in enumerate(sizes)],
        tokens, cotangent, down_a, up_b, slots,
    )


def solution(mesh):
    groups, n = mesh.shape["groups"], mesh.shape["tenant"]
    return jax.shard_map(
        functools.partial(shards, groups, n),
        mesh=mesh,
        in_specs=(
            P(("groups", "tenant"), None),
            P(("groups", "tenant"), None),
            P("tenant", None, None),
            P("tenant", None, None),
            P("groups"),
            P(),
        ),
        out_specs=(
            P(("groups", "tenant"), None),
            P(("groups", "tenant"), None, None),
            P(("groups", "tenant"), None, None),
        ),
        check_vma=False,
    )
```

```python
import functools

import jax
import jax.numpy as jnp
from jax import lax
from jax.experimental import pallas as pl
from jax.experimental.pallas import tpu as pltpu
from jax.sharding import PartitionSpec as P

adapter_scale = 2.0
MOST = 4
PIECES = 4
Q = 2 * PIECES
MESH = pl.DeviceIdType.MESH


def wait_bytes(ref, sem):
    pltpu.make_async_copy(ref, ref, sem).wait()


def kernel(
    groups, n, most_sent,
    tok_h, cot_h, down_h, up_h, slot_s,
    gt_h, gd_h, gu_h,
    raw, low, recv1, stage2, recv2, stage3, recv3, stage4, recv4, stage5,
    tok_v, cot_v, gt_v, own_s, pack_s, got_s, found_s, rank_s,
    in_sem, send_sem, recv_sem, gt_sem,
):
    width = tok_h.shape[1]
    block_rows = tok_h.shape[0]
    rank = down_h.shape[1]
    rows = rank // PIECES
    w = width // n
    ng = n // groups
    g = lax.axis_index("groups")
    me = lax.axis_index("tenant")
    side = me // ng
    r_me = me % ng
    c_me = g * ng + r_me
    crossing = (groups - 1) * most_sent

    def cols(c):
        return pl.ds(pl.multiple_of(c * w, w), w)

    share = pl.ds(pl.multiple_of(g * (ng * w), ng * w), ng * w)
    loads = [
        pltpu.make_async_copy(up_h.at[0, :, share], raw.at[0], in_sem.at[0]),
        pltpu.make_async_copy(down_h.at[0, :, share], raw.at[1], in_sem.at[1]),
        pltpu.make_async_copy(cot_h, cot_v, in_sem.at[2]),
        pltpu.make_async_copy(tok_h, tok_v, in_sem.at[3]),
    ]
    for load in loads:
        load.start()

    barrier = pltpu.get_barrier_semaphore()

    @pl.loop(1, n)
    def _(k):
        pl.semaphore_signal(barrier, inc=1, device_id=(g, (me + k) % n), device_id_type=MESH)

    for dg in range(1, groups):
        @pl.loop(0, ng)
        def _(r):
            pl.semaphore_signal(
                barrier, inc=1, device_id=((g + dg) % groups, side * ng + r), device_id_type=MESH
            )

    def cast(q):
        first = q % PIECES
        if first == 0:
            loads[q // PIECES].wait()

        @pl.loop(0, ng)
        def _(r):
            low[q, r] = raw[q // PIECES, pl.ds(first * rows, rows), cols(r)].astype(jnp.bfloat16)

    cast(0)
    for q in range(Q):
        recv3[q][n] = jnp.zeros((rows, w), jnp.bfloat16)
        recv4[q][crossing] = jnp.zeros((rows, w), jnp.bfloat16)
    pl.semaphore_wait(barrier, n - 1 + (groups - 1) * ng)

    def send(here, src, dst, hop, q, device):
        @pl.when(here)
        def _():
            pltpu.make_async_copy(src, dst, recv_sem.at[hop, q]).start()

        @pl.when(jnp.logical_not(here))
        def _():
            pltpu.make_async_remote_copy(
                src_ref=src, dst_ref=dst, send_sem=send_sem.at[hop, q], recv_sem=recv_sem.at[hop, q],
                device_id=device, device_id_type=MESH,
            ).start()

    def hop1(q):
        @pl.loop(0, n)
        def _(k):
            to = ((side + 1 + k // ng) % groups) * ng + (r_me + k) % ng
            send(to == me, low.at[q, to % ng], recv1[q].at[me], 0, q, (g, to))

    hop1(0)
    for q in range(1, Q):
        cast(q)
        hop1(q)

    def over_side(body):
        for dg in range(groups):
            @pl.loop(0, ng)
            def _(k):
                r = (r_me + k) % ng
                body((k == 0) if dg == 0 else (k < 0), dg, (g + dg) % groups, r)

    def hop2(q):
        wait_bytes(recv1[q], recv_sem.at[0, q])

        def one(here, dg, to_g, r):
            to = side * ng + r
            at = dg * ng + r
            stage2[q, at] = recv1[q][slot_s[dg, to]]
            send(here, stage2.at[q, at], recv2.at[q, c_me], 1, q, (to_g, to))

        over_side(one)

    hop2(0)

    def find(dg, t, base):
        def step(b, found):
            hit = slot_s[dg, base * ng + b] == t
            later = (((g + dg) % groups) * ng + b,) + found[:-1]
            return tuple(jnp.where(hit, new, old) for new, old in zip(later, found))
        return lax.fori_loop(0, ng, step, (jnp.int32(n),) * MOST)

    @pl.loop(0, n)
    def _(p):
        for i, b in enumerate(find(p // ng, side * ng + p % ng, side)):
            own_s[p * MOST + i] = b

    for i in range(MOST):
        found_s[n * MOST + i] = jnp.int32(n)
    for dh in range(1, groups):
        there, origin = (side + dh) % groups, (side + groups - dh) % groups

        def outgoing(p, count):
            found = find(p // ng, there * ng + p % ng, side)
            for i, b in enumerate(found):
                found_s[p * MOST + i] = b
            rank_s[p] = jnp.where(found[0] != n, count, -1)
            return count + jnp.where(found[0] != n, 1, 0)

        lax.fori_loop(0, n, outgoing, jnp.int32(0))

        @pl.loop(0, most_sent)
        def _(k):
            chosen = lax.fori_loop(
                0, n, lambda p, old: jnp.where(rank_s[p] == k, p, old), jnp.int32(n)
            )
            for i in range(MOST):
                pack_s[((dh - 1) * most_sent + k) * MOST + i] = found_s[chosen * MOST + i]

        def incoming(p, count):
            present = find(p // ng, side * ng + p % ng, origin)[0] != n
            got_s[(dh - 1) * n + p] = jnp.where(present, (dh - 1) * most_sent + count, crossing)
            return count + jnp.where(present, 1, 0)

        lax.fori_loop(0, n, incoming, jnp.int32(0))

    def rank_rows(rows_v, q):
        def step(c, total):
            return total + lax.dot_general(
                rows_v[:, cols(c)], recv2[q, c], (((1,), (1,)), ((), ())),
                preferred_element_type=jnp.float32,
            )
        return lax.fori_loop(0, n, step, jnp.zeros((block_rows, rows), jnp.float32))

    def hop3(q, left, rows_v, scale):
        def one(here, dg, to_g, r):
            c = to_g * ng + r
            term = scale * jnp.dot(left, rows_v[:, cols(c)], preferred_element_type=jnp.float32)
            stage3[q, c] = term.astype(jnp.bfloat16)
            send(here, stage3.at[q, c], recv3[q].at[c_me], 2, q, (to_g, side * ng + r))

        over_side(one)

    def block_sum(q, index_s, at):
        total = recv3[q][index_s[at]].astype(jnp.float32)
        for i in range(1, MOST):
            total += recv3[q][index_s[at + i]].astype(jnp.float32)
        return total

    def hop4(q):
        wait_bytes(recv3[q].at[pl.ds(0, n)], recv_sem.at[2, q])
        for dh in range(1, groups):
            to = ((side + dh) % groups) * ng + r_me

            @pl.loop(0, most_sent)
            def _(k):
                at = (dh - 1) * most_sent + k
                stage4[q, at] = block_sum(q, pack_s, at * MOST).astype(jnp.bfloat16)
                pltpu.make_async_remote_copy(
                    src_ref=stage4.at[q, at], dst_ref=recv4[q].at[at],
                    send_sem=send_sem.at[3, q], recv_sem=recv_sem.at[3, q],
                    device_id=(g, to), device_id_type=MESH,
                ).start()

    def home(q):
        out_h = gu_h if q >= PIECES else gd_h
        return out_h.at[0, pl.ds(q % PIECES * rows, rows)]

    def hop5(q):
        if groups > 1:
            wait_bytes(recv4[q].at[pl.ds(0, crossing)], recv_sem.at[3, q])

        def one(here, dg, to_g, r):
            p = dg * ng + r
            total = block_sum(q, own_s, p * MOST)
            for dh in range(1, groups):
                total += recv4[q][got_s[(dh - 1) * n + p]].astype(jnp.float32)
            stage5[q, p] = total.astype(jnp.bfloat16)
            send(here, stage5.at[q, p], home(q).at[:, cols(c_me)], 4, q, (to_g, side * ng + r))

        over_side(one)

    backward = []

    def ranks(q):
        wait_bytes(recv2.at[q], recv_sem.at[1, q])
        if q == 0:
            loads[2].wait()
            loads[3].wait()
        if q < PIECES:
            found = adapter_scale * rank_rows(cot_v, q)
            backward.append(found.astype(jnp.bfloat16))
            hop3(q, found.T.astype(jnp.bfloat16), tok_v, 1.0)
        else:
            hop3(q, rank_rows(tok_v, q).T.astype(jnp.bfloat16), cot_v, adapter_scale)

    gt_out = pltpu.make_async_copy(gt_v, gt_h, gt_sem)
    for at in range(Q + 3):
        if 0 < at < Q:
            hop2(at)
        if 0 <= at - 1 < Q:
            ranks(at - 1)
        if 0 <= at - 2 < Q:
            hop4(at - 2)
        if at == Q:
            @pl.loop(0, n)
            def _(c):
                total = jnp.zeros((block_rows, w), jnp.float32)
                for i in range(PIECES):
                    total += jnp.dot(
                        backward[i], recv2[PIECES + i, c], preferred_element_type=jnp.float32
                    )
                gt_v[:, cols(c)] = total.astype(jnp.bfloat16)

            gt_out.start()
        if 0 <= at - 3 < Q:
            hop5(at - 3)

    for q in range(Q):
        wait_bytes(home(q), recv_sem.at[4, q])
    for hop, source in ((0, stage2), (1, stage2), (2, stage3), (4, stage5)):
        for q in range(Q):
            wait_bytes(source.at[q, pl.ds(0, n - 1)], send_sem.at[hop, q])
    if groups > 1:
        for q in range(Q):
            wait_bytes(stage4.at[q], send_sem.at[3, q])
    gt_out.wait()


def adapters(groups, n, most_sent, name, tokens, cotangent, down_a, up_b, slots):
    block_rows, width = tokens.shape
    rank = down_a.shape[1]
    rows = rank // PIECES
    w = width // n
    ng = n // groups
    crossing = (groups - 1) * most_sent
    low = jnp.bfloat16
    whole = pl.BlockSpec(memory_space=pl.ANY)
    return pl.pallas_call(
        functools.partial(kernel, groups, n, most_sent),
        out_shape=(
            jax.ShapeDtypeStruct((block_rows, width), low),
            jax.ShapeDtypeStruct((1, rank, width), low),
            jax.ShapeDtypeStruct((1, rank, width), low),
        ),
        in_specs=[whole] * 4 + [pl.BlockSpec(memory_space=pltpu.SMEM)],
        out_specs=(whole,) * 3,
        scratch_shapes=[
            pltpu.VMEM((2, rank, ng * w), jnp.float32),
            pltpu.VMEM((Q, ng, rows, w), low),
            [pltpu.VMEM((n, rows, w), low)] * Q,
            pltpu.VMEM((Q, n, rows, w), low),
            pltpu.VMEM((Q, n, rows, w), low),
            pltpu.VMEM((Q, n, rows, w), low),
            [pltpu.VMEM((n + 1, rows, w), low)] * Q,
            pltpu.VMEM((Q, max(crossing, 1), rows, w), low),
            [pltpu.VMEM((crossing + 1, rows, w), low)] * Q,
            pltpu.VMEM((Q, n, rows, w), low),
            pltpu.VMEM((block_rows, width), low),
            pltpu.VMEM((block_rows, width), low),
            pltpu.VMEM((block_rows, width), low),
            pltpu.SMEM((n * MOST,), jnp.int32),
            pltpu.SMEM((max(crossing, 1) * MOST,), jnp.int32),
            pltpu.SMEM((max(groups - 1, 1) * n,), jnp.int32),
            pltpu.SMEM(((n + 1) * MOST,), jnp.int32),
            pltpu.SMEM((n,), jnp.int32),
            pltpu.SemaphoreType.DMA((4,)),
            pltpu.SemaphoreType.DMA((5, Q)),
            pltpu.SemaphoreType.DMA((5, Q)),
            pltpu.SemaphoreType.DMA,
        ],
        compiler_params=pltpu.CompilerParams(
            collective_id=name, has_side_effects=True, vmem_limit_bytes=56 * 2**20
        ),
    )(tokens, cotangent, down_a, up_b, slots)


def shards(groups, n, tokens, cotangent, down_a, up_b, block_tenant, tenant_slot):
    assert down_a.shape[0] == 1 and block_tenant.shape[0] == n
    ng = n // groups
    mine = tenant_slot[block_tenant]
    slots = jnp.stack([mine] + [
        lax.ppermute(mine, "groups", [((i + dg) % groups, i) for i in range(groups)])
        for dg in range(1, groups)
    ])
    hit = slots[:, :, None] == jnp.arange(n, dtype=jnp.int32)
    pairs = jnp.any(hit.reshape(groups, groups, ng, groups, ng), axis=2)
    apart = jnp.arange(groups)[:, None] != jnp.arange(groups)[None, :]
    most = jnp.max(jnp.sum(pairs & apart[None, :, :, None], axis=(0, 3), dtype=jnp.int32))
    sizes = sorted({n // 2, n * 5 // 8, n})
    which = sum((most > size).astype(jnp.int32) for size in sizes[:-1])
    return lax.switch(
        which,
        [functools.partial(adapters, groups, n, size, i) for i, size in enumerate(sizes)],
        tokens, cotangent, down_a, up_b, slots,
    )


def solution(mesh):
    groups, n = mesh.shape["groups"], mesh.shape["tenant"]
    return jax.shard_map(
        functools.partial(shards, groups, n),
        mesh=mesh,
        in_specs=(
            P(("groups", "tenant"), None),
            P(("groups", "tenant"), None),
            P("tenant", None, None),
            P("tenant", None, None),
            P("groups"),
            P(),
        ),
        out_specs=(
            P(("groups", "tenant"), None),
            P(("groups", "tenant"), None, None),
            P(("groups", "tenant"), None, None),
        ),
        check_vma=False,
    )
```

```python
import functools

import jax
import jax.numpy as jnp
from jax import lax
from jax.experimental import pallas as pl
from jax.experimental.pallas import tpu as pltpu
from jax.sharding import PartitionSpec as P

adapter_scale = 2.0
MOST = 4
PIECES = 2
Q = 2 * PIECES
MESH = pl.DeviceIdType.MESH


def wait_bytes(ref, sem):
    pltpu.make_async_copy(ref, ref, sem).wait()


def kernel(
    groups, n, most_sent,
    tok_h, cot_h, down_h, up_h, slot_s,
    gt_h, gd_h, gu_h,
    raw, low, recv1, stage2, recv2, stage3, recv3, stage4, recv4, stage5,
    tok_v, cot_v, gt_v, own_s, pack_s, got_s, found_s, rank_s,
    in_sem, send_sem, recv_sem, gt_sem,
):
    width = tok_h.shape[1]
    block_rows = tok_h.shape[0]
    rank = down_h.shape[1]
    rows = rank // PIECES
    w = width // n
    ng = n // groups
    g = lax.axis_index("groups")
    me = lax.axis_index("tenant")
    side = me // ng
    r_me = me % ng
    c_me = g * ng + r_me
    crossing = (groups - 1) * most_sent

    def cols(c):
        return pl.ds(pl.multiple_of(c * w, w), w)

    share = pl.ds(pl.multiple_of(g * (ng * w), ng * w), ng * w)
    loads = [
        pltpu.make_async_copy(up_h.at[0, :, share], raw.at[0], in_sem.at[0]),
        pltpu.make_async_copy(down_h.at[0, :, share], raw.at[1], in_sem.at[1]),
        pltpu.make_async_copy(cot_h, cot_v, in_sem.at[2]),
        pltpu.make_async_copy(tok_h, tok_v, in_sem.at[3]),
    ]
    for load in loads:
        load.start()

    barrier = pltpu.get_barrier_semaphore()

    @pl.loop(1, n)
    def _(k):
        pl.semaphore_signal(barrier, inc=1, device_id=(g, (me + k) % n), device_id_type=MESH)

    for dg in range(1, groups):
        @pl.loop(0, ng)
        def _(r):
            pl.semaphore_signal(
                barrier, inc=1, device_id=((g + dg) % groups, side * ng + r), device_id_type=MESH
            )

    def cast(q):
        first = q % PIECES
        if first == 0:
            loads[q // PIECES].wait()

        @pl.loop(0, ng)
        def _(r):
            low[q, r] = raw[q // PIECES, pl.ds(first * rows, rows), cols(r)].astype(jnp.bfloat16)

    cast(0)
    for q in range(Q):
        recv3[q][n] = jnp.zeros((rows, w), jnp.bfloat16)
        recv4[q][crossing] = jnp.zeros((rows, w), jnp.bfloat16)
    pl.semaphore_wait(barrier, n - 1 + (groups - 1) * ng)

    def send(here, src, dst, hop, q, device):
        @pl.when(here)
        def _():
            pltpu.make_async_copy(src, dst, recv_sem.at[hop, q]).start()

        @pl.when(jnp.logical_not(here))
        def _():
            pltpu.make_async_remote_copy(
                src_ref=src, dst_ref=dst, send_sem=send_sem.at[hop, q], recv_sem=recv_sem.at[hop, q],
                device_id=device, device_id_type=MESH,
            ).start()

    def hop1(q):
        @pl.loop(0, n)
        def _(k):
            to = ((side + 1 + k // ng) % groups) * ng + (r_me + k) % ng
            send(to == me, low.at[q, to % ng], recv1[q].at[me], 0, q, (g, to))

    hop1(0)
    for q in range(1, Q):
        cast(q)
        hop1(q)

    def over_side(body):
        for dg in range(groups):
            @pl.loop(0, ng)
            def _(k):
                r = (r_me + k) % ng
                body((k == 0) if dg == 0 else (k < 0), dg, (g + dg) % groups, r)

    def hop2(q):
        wait_bytes(recv1[q], recv_sem.at[0, q])

        def one(here, dg, to_g, r):
            to = side * ng + r
            at = dg * ng + r
            stage2[q, at] = recv1[q][slot_s[dg, to]]
            send(here, stage2.at[q, at], recv2.at[q, c_me], 1, q, (to_g, to))

        over_side(one)

    hop2(0)

    def find(dg, t, base):
        def step(b, found):
            hit = slot_s[dg, base * ng + b] == t
            later = (((g + dg) % groups) * ng + b,) + found[:-1]
            return tuple(jnp.where(hit, new, old) for new, old in zip(later, found))
        return lax.fori_loop(0, ng, step, (jnp.int32(n),) * MOST)

    @pl.loop(0, n)
    def _(p):
        for i, b in enumerate(find(p // ng, side * ng + p % ng, side)):
            own_s[p * MOST + i] = b

    for i in range(MOST):
        found_s[n * MOST + i] = jnp.int32(n)
    for dh in range(1, groups):
        there, origin = (side + dh) % groups, (side + groups - dh) % groups

        def outgoing(p, count):
            found = find(p // ng, there * ng + p % ng, side)
            for i, b in enumerate(found):
                found_s[p * MOST + i] = b
            rank_s[p] = jnp.where(found[0] != n, count, -1)
            return count + jnp.where(found[0] != n, 1, 0)

        lax.fori_loop(0, n, outgoing, jnp.int32(0))

        @pl.loop(0, most_sent)
        def _(k):
            chosen = lax.fori_loop(
                0, n, lambda p, old: jnp.where(rank_s[p] == k, p, old), jnp.int32(n)
            )
            for i in range(MOST):
                pack_s[((dh - 1) * most_sent + k) * MOST + i] = found_s[chosen * MOST + i]

        def incoming(p, count):
            present = find(p // ng, side * ng + p % ng, origin)[0] != n
            got_s[(dh - 1) * n + p] = jnp.where(present, (dh - 1) * most_sent + count, crossing)
            return count + jnp.where(present, 1, 0)

        lax.fori_loop(0, n, incoming, jnp.int32(0))

    def rank_rows(rows_v, q):
        def step(c, total):
            return total + lax.dot_general(
                rows_v[:, cols(c)], recv2[q, c], (((1,), (1,)), ((), ())),
                preferred_element_type=jnp.float32,
            )
        return lax.fori_loop(0, n, step, jnp.zeros((block_rows, rows), jnp.float32))

    def hop3(q, left, rows_v, scale):
        def one(here, dg, to_g, r):
            c = to_g * ng + r
            term = scale * jnp.dot(left, rows_v[:, cols(c)], preferred_element_type=jnp.float32)
            stage3[q, c] = term.astype(jnp.bfloat16)
            send(here, stage3.at[q, c], recv3[q].at[c_me], 2, q, (to_g, side * ng + r))

        over_side(one)

    def block_sum(q, index_s, at):
        total = recv3[q][index_s[at]].astype(jnp.float32)
        for i in range(1, MOST):
            total += recv3[q][index_s[at + i]].astype(jnp.float32)
        return total

    def hop4(q):
        wait_bytes(recv3[q].at[pl.ds(0, n)], recv_sem.at[2, q])
        for dh in range(1, groups):
            to = ((side + dh) % groups) * ng + r_me

            @pl.loop(0, most_sent)
            def _(k):
                at = (dh - 1) * most_sent + k
                stage4[q, at] = block_sum(q, pack_s, at * MOST).astype(jnp.bfloat16)
                pltpu.make_async_remote_copy(
                    src_ref=stage4.at[q, at], dst_ref=recv4[q].at[at],
                    send_sem=send_sem.at[3, q], recv_sem=recv_sem.at[3, q],
                    device_id=(g, to), device_id_type=MESH,
                ).start()

    def home(q):
        out_h = gu_h if q >= PIECES else gd_h
        return out_h.at[0, pl.ds(q % PIECES * rows, rows)]

    def hop5(q):
        if groups > 1:
            wait_bytes(recv4[q].at[pl.ds(0, crossing)], recv_sem.at[3, q])

        def one(here, dg, to_g, r):
            p = dg * ng + r
            total = block_sum(q, own_s, p * MOST)
            for dh in range(1, groups):
                total += recv4[q][got_s[(dh - 1) * n + p]].astype(jnp.float32)
            stage5[q, p] = total.astype(jnp.bfloat16)
            send(here, stage5.at[q, p], home(q).at[:, cols(c_me)], 4, q, (to_g, side * ng + r))

        over_side(one)

    backward = []

    def ranks(q):
        wait_bytes(recv2.at[q], recv_sem.at[1, q])
        if q == 0:
            loads[2].wait()
            loads[3].wait()
        if q < PIECES:
            found = adapter_scale * rank_rows(cot_v, q)
            backward.append(found.astype(jnp.bfloat16))
            hop3(q, found.T.astype(jnp.bfloat16), tok_v, 1.0)
        else:
            hop3(q, rank_rows(tok_v, q).T.astype(jnp.bfloat16), cot_v, adapter_scale)

    gt_out = pltpu.make_async_copy(gt_v, gt_h, gt_sem)
    for at in range(Q + 3):
        if 0 < at < Q:
            hop2(at)
        if 0 <= at - 1 < Q:
            ranks(at - 1)
        if 0 <= at - 2 < Q:
            hop4(at - 2)
        if at == Q:
            @pl.loop(0, n)
            def _(c):
                total = jnp.zeros((block_rows, w), jnp.float32)
                for i in range(PIECES):
                    total += jnp.dot(
                        backward[i], recv2[PIECES + i, c], preferred_element_type=jnp.float32
                    )
                gt_v[:, cols(c)] = total.astype(jnp.bfloat16)

            gt_out.start()
        if 0 <= at - 3 < Q:
            hop5(at - 3)

    for q in range(Q):
        wait_bytes(home(q), recv_sem.at[4, q])
    for hop, source in ((0, stage2), (1, stage2), (2, stage3), (4, stage5)):
        for q in range(Q):
            wait_bytes(source.at[q, pl.ds(0, n - 1)], send_sem.at[hop, q])
    if groups > 1:
        for q in range(Q):
            wait_bytes(stage4.at[q], send_sem.at[3, q])
    gt_out.wait()


def adapters(groups, n, most_sent, name, tokens, cotangent, down_a, up_b, slots):
    block_rows, width = tokens.shape
    rank = down_a.shape[1]
    rows = rank // PIECES
    w = width // n
    ng = n // groups
    crossing = (groups - 1) * most_sent
    low = jnp.bfloat16
    whole = pl.BlockSpec(memory_space=pl.ANY)
    return pl.pallas_call(
        functools.partial(kernel, groups, n, most_sent),
        out_shape=(
            jax.ShapeDtypeStruct((block_rows, width), low),
            jax.ShapeDtypeStruct((1, rank, width), low),
            jax.ShapeDtypeStruct((1, rank, width), low),
        ),
        in_specs=[whole] * 4 + [pl.BlockSpec(memory_space=pltpu.SMEM)],
        out_specs=(whole,) * 3,
        scratch_shapes=[
            pltpu.VMEM((2, rank, ng * w), jnp.float32),
            pltpu.VMEM((Q, ng, rows, w), low),
            [pltpu.VMEM((n, rows, w), low)] * Q,
            pltpu.VMEM((Q, n, rows, w), low),
            pltpu.VMEM((Q, n, rows, w), low),
            pltpu.VMEM((Q, n, rows, w), low),
            [pltpu.VMEM((n + 1, rows, w), low)] * Q,
            pltpu.VMEM((Q, max(crossing, 1), rows, w), low),
            [pltpu.VMEM((crossing + 1, rows, w), low)] * Q,
            pltpu.VMEM((Q, n, rows, w), low),
            pltpu.VMEM((block_rows, width), low),
            pltpu.VMEM((block_rows, width), low),
            pltpu.VMEM((block_rows, width), low),
            pltpu.SMEM((n * MOST,), jnp.int32),
            pltpu.SMEM((max(crossing, 1) * MOST,), jnp.int32),
            pltpu.SMEM((max(groups - 1, 1) * n,), jnp.int32),
            pltpu.SMEM(((n + 1) * MOST,), jnp.int32),
            pltpu.SMEM((n,), jnp.int32),
            pltpu.SemaphoreType.DMA((4,)),
            pltpu.SemaphoreType.DMA((5, Q)),
            pltpu.SemaphoreType.DMA((5, Q)),
            pltpu.SemaphoreType.DMA,
        ],
        compiler_params=pltpu.CompilerParams(
            collective_id=name, has_side_effects=True, vmem_limit_bytes=56 * 2**20
        ),
    )(tokens, cotangent, down_a, up_b, slots)


def shards(groups, n, tokens, cotangent, down_a, up_b, block_tenant, tenant_slot):
    assert down_a.shape[0] == 1 and block_tenant.shape[0] == n
    ng = n // groups
    mine = tenant_slot[block_tenant]
    slots = jnp.stack([mine] + [
        lax.ppermute(mine, "groups", [((i + dg) % groups, i) for i in range(groups)])
        for dg in range(1, groups)
    ])
    hit = slots[:, :, None] == jnp.arange(n, dtype=jnp.int32)
    pairs = jnp.any(hit.reshape(groups, groups, ng, groups, ng), axis=2)
    apart = jnp.arange(groups)[:, None] != jnp.arange(groups)[None, :]
    most = jnp.max(jnp.sum(pairs & apart[None, :, :, None], axis=(0, 3), dtype=jnp.int32))
    sizes = sorted({n * 3 // 8, n * 7 // 16, n // 2, n * 5 // 8, n})
    which = sum((most > size).astype(jnp.int32) for size in sizes[:-1])
    return lax.switch(
        which,
        [functools.partial(adapters, groups, n, size, i) for i, size in enumerate(sizes)],
        tokens, cotangent, down_a, up_b, slots,
    )


def solution(mesh):
    groups, n = mesh.shape["groups"], mesh.shape["tenant"]
    return jax.shard_map(
        functools.partial(shards, groups, n),
        mesh=mesh,
        in_specs=(
            P(("groups", "tenant"), None),
            P(("groups", "tenant"), None),
            P("tenant", None, None),
            P("tenant", None, None),
            P("groups"),
            P(),
        ),
        out_specs=(
            P(("groups", "tenant"), None),
            P(("groups", "tenant"), None, None),
            P(("groups", "tenant"), None, None),
        ),
        check_vma=False,
    )
```
